32 devices in a mesh: gx: 8 (over z, core), gy: 4 (over y, x).
Axes of the slice: x: 2, y: 2, z: 4, core: 2. Of those that a mesh axis runs over, the one named last changes fastest.
Arguments:
- directions: float32 [16, 128, 128, 128], P(None, 'gx', 'gy'), may hold values from -6 to 6
- checkpoints: float32 [16, 128, 128, 128], P(None, 'gx', 'gy'), may hold values from -3 to 3
- restart: int32 [1], replicated, may hold values from 0 to 15
- diffusivity: float32 [128, 128, 128], P('gx', 'gy'), may hold values from 0.5 to 1.5
- velocity: float32 [3], replicated, may hold values from -0.4 to 0.4
- weights: float32 [128, 128, 128], P('gx', 'gy'), may hold values from 0.25 to 4
Outputs:
- basis: float32 [16, 128, 128, 128], P(None, 'gx', 'gy')
- factor: float32 [16, 16], replicated
The draws below stay inside these ranges and needn't reach their ends.
All inputs are finite; a program needn't handle non-finite values.
Results may differ from the reference program's by a relative error of at most 0.0003.
Values sent between devices are 32-bit elements; how exact they have to be, the bound alone decides.
A program may use at most 128 MiB of HBM per device.

```python
import math
import jax
import jax.numpy as jnp
from jax import lax

K = 16
NZ = 128
NCK = 16
NX = 128
NY = 128


def mixing(key, count, strength):
    key_along, key_noise = jax.random.split(key)
    along = jax.random.normal(key_along, (count,), jnp.float32)
    noise = jax.random.normal(key_noise, (count, count), jnp.float32)
    common = jnp.dot(noise, noise.T, precision=lax.Precision.HIGHEST) / count
    matrix = jnp.eye(count, dtype=jnp.float32) + strength * along[:, None] * along[None, :] + 0.5 * common
    lengths = jnp.sqrt(jnp.sum(matrix * matrix, axis=1, keepdims=True))
    return matrix / lengths


def draw_directions(key, part):
    key = jax.random.fold_in(key, 11)
    key_mix, key_field = jax.random.split(key, 2)
    fields = jax.random.truncated_normal(key_field, -4.0, 4.0, (K, NX, NY, NZ), jnp.float32)
    matrix = mixing(key_mix, K, 0.3)
    mixed = jnp.einsum('kj,jxyz->kxyz', matrix, fields, precision=lax.Precision.HIGHEST)
    return jnp.clip(mixed, -6.0, 6.0)


def block_scale(rng, extent, cuts, low, largest):
    gain = 1.0
    for axis_at, parts in cuts:
        draws = jax.random.uniform(jax.random.fold_in(jax.random.fold_in(rng, 6), axis_at), (parts,), jnp.float32, low / len(cuts), largest / len(cuts))
        gain = gain * jnp.repeat(jnp.exp(draws), extent[axis_at] // parts).reshape((-1,) + (1,) * (len(extent) - 1 - axis_at))
    return gain


def bell_draw(key, extent, width, most, cuts=(), held_as=jnp.bfloat16):
    values = width * jax.random.normal(key, extent, jnp.float32)
    if cuts:
        values = values * block_scale(key, extent, cuts, -0.22, 0.18)
    return jnp.clip(values, -most, most).astype(held_as)


def setup_inputs(seed: int = 0) -> dict:
    key_of = jax.random.split(jax.random.key(seed), 7)
    return {
        "directions": draw_directions(jax.random.fold_in(key_of[6], 71), 0),
        "checkpoints": bell_draw(key_of[1], (NCK, NX, NY, NZ), 1.0, 3.0, ((1, 8), (2, 4)), jnp.float32),
        "restart": jax.random.randint(key_of[2], (1,), 0, NCK).astype(jnp.int32),
        "diffusivity": jnp.clip(0.5 + 1.0 * jax.random.uniform(key_of[3], (NX, NY, NZ), jnp.float32) ** block_scale(key_of[3], (NX, NY, NZ), ((0, 8), (1, 4)), -0.2, 0.2), 0.5, 1.5),
        "velocity": jnp.clip(jax.random.uniform(key_of[4], (3,), jnp.float32, -0.4, 0.4), -0.4, 0.4),
        "weights": jnp.clip(jnp.exp(math.log(4.0) - 2.7725887 * jax.random.uniform(key_of[5], (NX, NY, NZ), jnp.float32) ** block_scale(key_of[5], (NX, NY, NZ), ((0, 8), (1, 4)), -0.2, 0.2)), 0.25, 4.0),
    }


DIFFUSE = 0.1
REACT = 0.05
PRIOR = 0.25

def pad_plane(field):
    return jnp.pad(field, [(0, 0)] * (field.ndim - 3) + [(1, 1), (1, 1), (0, 0)])

def stencil(field, velocity):
    padded = jnp.pad(field, [(0, 0)] * (field.ndim - 1) + [(1, 1)])
    middle = field[..., 1:-1, 1:-1, :]
    east = field[..., 2:, 1:-1, :]
    west = field[..., :-2, 1:-1, :]
    north = field[..., 1:-1, 2:, :]
    south = field[..., 1:-1, :-2, :]
    upper = padded[..., 1:-1, 1:-1, 2:]
    lower = padded[..., 1:-1, 1:-1, :-2]
    laplace = east + west + north + south + upper + lower - 6.0 * middle
    advect = 0.5 * (velocity[0] * (east - west) + velocity[1] * (north - south) + velocity[2] * (upper - lower))
    return (middle, laplace, advect)

def advance(state, diffusivity, velocity):
    middle, laplace, advect = stencil(pad_plane(state), velocity)
    return middle + DIFFUSE * diffusivity * laplace - advect - REACT * middle * middle * middle

def tangent(field, state, diffusivity, velocity):
    middle, laplace, advect = stencil(pad_plane(field), velocity)
    return middle + DIFFUSE * diffusivity * laplace - advect - 3.0 * REACT * state * state * middle

def adjoint(field, state, diffusivity, velocity):
    unused, laplace, ignored = stencil(pad_plane(diffusivity * field), velocity)
    middle, nothing, advect = stencil(pad_plane(field), velocity)
    return middle + DIFFUSE * laplace + advect - 3.0 * REACT * state * state * middle

def reference(directions, checkpoints, restart, diffusivity, velocity, weights):
    start = lax.dynamic_index_in_dim(checkpoints, restart[0].astype(jnp.int32), 0, keepdims=False)
    later = advance(start, diffusivity, velocity)

    def single(direction):
        first = tangent(direction, start, diffusivity, velocity)
        second = tangent(first, later, diffusivity, velocity)
        back_one = adjoint(weights * second, later, diffusivity, velocity)
        back_two = adjoint(back_one, start, diffusivity, velocity)
        return back_two + PRIOR * direction
    sketch = lax.map(single, directions)
    flat = sketch.reshape(K, -1)
    cells = jnp.float32(NX * NY * NZ)
    gram = jnp.dot(flat, flat.T, precision=lax.Precision.HIGHEST) / cells
    lower_factor = jnp.linalg.cholesky(gram)
    solved = lax.linalg.triangular_solve(lower_factor, flat, left_side=True, lower=True)
    return (solved.reshape(sketch.shape), lower_factor.T)
```

```python
import functools

import jax
import jax.numpy as jnp
from jax import lax
from jax.experimental import pallas as pl
from jax.experimental.pallas import tpu as pltpu
from jax.sharding import PartitionSpec as P

DIFFUSE = 0.1
REACT = 0.05
PRIOR = 0.25
GROUP = 4
MESH = pl.DeviceIdType.MESH
HIGHEST = lax.Precision.HIGHEST


def iota(shape, dim):
    return lax.broadcasted_iota(jnp.int32, shape, dim)


def sketch_kernel(
    nx, ny, cells,
    velocity, directions, start_in, diffusivity_in, weights_in,
    sketch, mixer, factor,
    f0, f1, f2, f3, pair, wts, ct, ca, c0s, c0l,
    ysend, yrecv, ypsend, yprecv, gram_x, gram_y,
    local_sem, send_sem, recv_sem, psend_sem, precv_sem, gsend_sem, grecv_sem,
):
    fields = (f0, f1, f2, f3)
    k_all, lx, ly, lz = sketch.shape
    tiles = ly // 8
    groups = k_all // GROUP
    gx, gy = lax.axis_index("gx"), lax.axis_index("gy")

    barrier = pltpu.get_barrier_semaphore()
    for axis, me, count in (("gx", gx, nx), ("gy", gy, ny)):
        for step in range(1, count):
            pl.semaphore_signal(
                barrier, inc=1, device_id={axis: lax.rem(me + step, count)}, device_id_type=MESH
            )

    def load_group(c):
        ks = pl.ds(c * GROUP, GROUP)
        return pltpu.make_async_copy(
            directions.at[ks], f0.at[ks, pl.ds(1, lx)], local_sem.at[c]
        )

    side_copies = (
        pltpu.make_async_copy(start_in, pair.at[0, pl.ds(1, lx)], local_sem.at[groups]),
        pltpu.make_async_copy(diffusivity_in, pair.at[1, pl.ds(1, lx)], local_sem.at[groups + 1]),
        pltpu.make_async_copy(weights_in, wts, local_sem.at[groups + 2]),
    )
    load_group(0).start()
    side_copies[0].start()
    side_copies[1].start()
    for c in range(1, groups):
        load_group(c).start()
    side_copies[2].start()

    plane_zero = jnp.zeros((ly, lz), jnp.float32)
    row_zero = jnp.zeros((lx, lz), jnp.float32)

    for edge, where in ((gx == 0, 0), (gx == nx - 1, lx + 1)):
        @pl.when(edge)
        def _(where=where):
            @pl.loop(0, k_all)
            def _(k):
                for field in fields:
                    field[k, where] = plane_zero
            for k in range(2):
                pair[k, where] = plane_zero

    for edge, side in ((gy == 0, 0), (gy == ny - 1, 1)):
        @pl.when(edge)
        def _(side=side):
            @pl.loop(0, k_all)
            def _(k):
                for stage in range(4):
                    yrecv[stage, side, k] = row_zero
            for k in range(2):
                yprecv[side, k] = row_zero

    def routes(planes, ys, yr, ks, send, recv):
        def copy(src, dst, side, peer):
            return pltpu.make_async_remote_copy(
                src_ref=src, dst_ref=dst, send_sem=send(side), recv_sem=recv(side),
                device_id=peer, device_id_type=MESH,
            )
        return (
            (gx < nx - 1, gx > 0, copy(planes.at[ks, lx], planes.at[ks, 0], 0, {"gx": lax.rem(gx + 1, nx)})),
            (gx > 0, gx < nx - 1, copy(planes.at[ks, 1], planes.at[ks, lx + 1], 1, {"gx": lax.rem(gx + nx - 1, nx)})),
            (gy < ny - 1, gy > 0, copy(ys.at[0, ks], yr.at[0, ks], 2, {"gy": lax.rem(gy + 1, ny)})),
            (gy > 0, gy < ny - 1, copy(ys.at[1, ks], yr.at[1, ks], 3, {"gy": lax.rem(gy + ny - 1, ny)})),
        )

    def stage_routes(stage, c):
        return routes(
            fields[stage], ysend.at[stage], yrecv.at[stage], pl.ds(c * GROUP, GROUP),
            lambda side: send_sem.at[stage, side, c], lambda side: recv_sem.at[stage, side, c],
        )

    def pair_routes():
        return routes(
            pair, ypsend, yprecv, pl.ds(0, 2),
            lambda side: psend_sem.at[side], lambda side: precv_sem.at[side],
        )

    def send_all(ways):
        for sends, _, copy in ways:
            pl.when(sends)(copy.start)

    def recv_all(ways):
        for _, receives, copy in ways:
            pl.when(receives)(copy.wait_recv)

    def sent_all(ways):
        for sends, _, copy in ways:
            pl.when(sends)(copy.wait_send)

    row = iota((8, lz), 0)
    lane = iota((8, lz), 1)
    hx, hy, hz = (0.5 * velocity[i] for i in range(3))

    def around(field, yr, k, x, t):
        p = x + 1
        lo = t * 8
        middle = field[k, p, lo:lo + 8, :]
        east = field[k, p + 1, lo:lo + 8, :]
        west = field[k, p - 1, lo:lo + 8, :]
        if t < tiles - 1:
            north = field[k, p, lo + 1:lo + 9, :]
        else:
            north = jnp.where(row == 7, yr[1, k, pl.ds(x, 1), :], pltpu.roll(middle, 7, 0))
        if t > 0:
            south = field[k, p, lo - 1:lo + 7, :]
        else:
            south = jnp.where(row == 0, yr[0, k, pl.ds(x, 1), :], pltpu.roll(middle, 1, 0))
        upper = pltpu.roll(middle, lz - 1, 1)
        lower = pltpu.roll(middle, 1, 1)
        return middle, (east, west, north, south, upper, lower)

    def weighted(c0, cs, middle, sides):
        terms = [c * v for c, v in zip(cs, sides)]
        return ((terms[0] + terms[1]) + (terms[2] + terms[3])) + ((terms[4] + terms[5]) + c0 * middle)

    def pack_group(c):
        @pl.loop(0, lx)
        def _(x):
            for i in range(GROUP):
                k = c * GROUP + i
                ysend[0, 0, k, pl.ds(x, 1), :] = f0[k, x + 1, ly - 1:ly, :]
                ysend[0, 1, k, pl.ds(x, 1), :] = f0[k, x + 1, 0:1, :]

    load_group(0).wait()
    pack_group(0)
    side_copies[0].wait()
    side_copies[1].wait()

    @pl.loop(0, lx)
    def _(x):
        for k in range(2):
            ypsend[0, k, pl.ds(x, 1), :] = pair[k, x + 1, ly - 1:ly, :]
            ypsend[1, k, pl.ds(x, 1), :] = pair[k, x + 1, 0:1, :]

    pl.semaphore_wait(barrier, nx + ny - 2)
    send_all(stage_routes(0, 0))
    send_all(pair_routes())

    @pl.loop(1, groups)
    def _(c):
        load_group(c).wait()
        pack_group(c)
        send_all(stage_routes(0, c))

    @pl.loop(0, lx)
    def _(x):
        for t in range(tiles):
            rows = slice(t * 8, t * 8 + 8)
            a = DIFFUSE * pair[1, x + 1, rows, :]
            state = pair[0, x + 1, rows, :]
            ct[0, x, rows, :] = a - hx
            ct[1, x, rows, :] = a + hx
            ct[2, x, rows, :] = a - hy
            ct[3, x, rows, :] = a + hy
            ct[4, x, rows, :] = jnp.where(lane < lz - 1, a - hz, 0.0)
            ct[5, x, rows, :] = jnp.where(lane > 0, a + hz, 0.0)
            c0s[x, rows, :] = 1.0 - 6.0 * a - (3.0 * REACT) * state * state

    def run_stage(stage, coefs, centre, finish, out):
        field = fields[stage]
        last = stage == 3

        @pl.loop(0, groups)
        def _(c):
            recv_all(stage_routes(stage, c))

            @pl.loop(0, lx)
            def _(x):
                for t in range(tiles):
                    rows = slice(t * 8, t * 8 + 8)
                    cs = [coefs[i, x, rows, :] for i in range(6)]
                    c0 = centre[x, rows, :]
                    extra = wts[x, rows, :] if finish == "weights" else None
                    for i in range(GROUP):
                        k = c * GROUP + i
                        middle, sides = around(field, yrecv.at[stage], k, x, t)
                        value = weighted(c0, cs, middle, sides)
                        if finish == "weights":
                            value = extra * value
                        if finish == "prior":
                            value = value + PRIOR * f0[k, x + 1, rows, :]
                        if last:
                            out[k, x, rows, :] = value
                        else:
                            out[k, x + 1, rows, :] = value
                            if t == tiles - 1:
                                ysend[stage + 1, 0, k, pl.ds(x, 1), :] = value[7:8, :]
                            if t == 0:
                                ysend[stage + 1, 1, k, pl.ds(x, 1), :] = value[0:1, :]

            if not last:
                send_all(stage_routes(stage + 1, c))

    run_stage(0, ct, c0s, None, f1)

    recv_all(pair_routes())
    side_copies[2].wait()

    @pl.loop(0, lx)
    def _(x):
        for t in range(tiles):
            rows = slice(t * 8, t * 8 + 8)
            state, sides = around(pair, yprecv, 0, x, t)
            cs = [ct[i, x, rows, :] for i in range(6)]
            diff, around_diff = around(pair, yprecv, 1, x, t)
            plain = 1.0 - (6.0 * DIFFUSE) * diff
            later = weighted(plain - REACT * state * state, cs, state, sides)
            c0l[x, rows, :] = plain - (3.0 * REACT) * later * later
            for i, (speed, other) in enumerate(zip((hx, -hx, hy, -hy, hz, -hz), around_diff)):
                value = DIFFUSE * other + speed
                if i == 4:
                    value = jnp.where(lane < lz - 1, value, 0.0)
                if i == 5:
                    value = jnp.where(lane > 0, value, 0.0)
                ca[i, x, rows, :] = value

    run_stage(1, ct, c0l, "weights", f2)
    run_stage(2, ca, c0l, None, f3)
    run_stage(3, ca, c0s, "prior", sketch)

    side = k_all * 8

    def products(x, total):
        block = jnp.concatenate(
            [sketch[:, x, t * 8:t * 8 + 8, :].reshape(side, lz) for t in range(tiles)], axis=1
        )
        high = block.astype(jnp.bfloat16)
        low = (block - high.astype(jnp.float32)).astype(jnp.bfloat16)
        return total + lax.dot_general(
            high, jnp.concatenate([high, low], axis=0), (((1,), (1,)), ((), ())),
            preferred_element_type=jnp.float32,
        )

    total = lax.fori_loop(0, lx, products, jnp.zeros((side, 2 * side), jnp.float32))
    low_part = total[:, side:]
    whole = total[:, :side] + low_part + low_part.T
    r_big, c_big = iota((side, side), 0), iota((side, side), 1)
    same_y = (r_big & 7) == (c_big & 7)
    whole = jnp.where(same_y, whole, 0.0)
    fold = (iota((k_all, side), 0) == iota((k_all, side), 1) >> 3).astype(jnp.float32)
    folded = jnp.dot(fold, whole, precision=HIGHEST, preferred_element_type=jnp.float32)

    for axis, me, count, slots, at in (("gx", gx, nx, gram_x, 0), ("gy", gy, ny, gram_y, nx)):
        slots[me] = folded
        copies = []
        for step in range(1, count):
            peer = lax.rem(me + step, count)
            copies.append(pltpu.make_async_remote_copy(
                src_ref=slots.at[me], dst_ref=slots.at[me],
                send_sem=gsend_sem.at[at + step], recv_sem=grecv_sem.at[at + me],
                device_id={axis: peer}, device_id_type=MESH,
            ))
        for copy in copies:
            copy.start()
        for step in range(1, count):
            peer = lax.rem(me + step, count)
            pltpu.make_async_remote_copy(
                src_ref=slots.at[peer], dst_ref=slots.at[peer],
                send_sem=gsend_sem.at[at + step], recv_sem=grecv_sem.at[at + peer],
                device_id={axis: peer}, device_id_type=MESH,
            ).wait_recv()
        folded = slots[0]
        for i in range(1, count):
            folded = folded + slots[i]
        for copy in copies:
            copy.wait_send()

    pick = (iota((side, lz), 0) >> 3 == iota((side, lz), 1)).astype(jnp.float32)
    work = jnp.dot(folded * (1.0 / cells), pick, precision=HIGHEST, preferred_element_type=jnp.float32)
    kr, kc = iota((k_all, lz), 0), iota((k_all, lz), 1)
    work = work + (kc == kr + k_all).astype(jnp.float32)
    for j in range(k_all - 1):
        ratio = jnp.where(kr > j, work[:, j:j + 1] / work[j:j + 1, j:j + 1], 0.0)
        work = work - ratio * work[j:j + 1, :]
    diagonal = jnp.sum(jnp.where(kr == kc, work, 0.0), axis=1, keepdims=True)
    work = work / jnp.sqrt(diagonal)
    factor[...] = jnp.where(kc >= kr, work, 0.0)[:, :k_all]
    spread = (iota((lz, side), 0) == (iota((lz, side), 1) >> 3) + k_all).astype(jnp.float32)
    inverse = jnp.dot(work, spread, precision=HIGHEST, preferred_element_type=jnp.float32)
    unfold = (iota((side, k_all), 0) >> 3 == iota((side, k_all), 1)).astype(jnp.float32)
    inverse = jnp.dot(unfold, inverse, precision=HIGHEST, preferred_element_type=jnp.float32)
    inverse = jnp.where(same_y, inverse, 0.0)
    high = inverse.astype(jnp.bfloat16)
    low = (inverse - high.astype(jnp.float32)).astype(jnp.bfloat16)
    mixer[:side, :side] = high
    mixer[:side, side:] = high
    mixer[side:, :side] = low
    mixer[side:, side:] = jnp.zeros_like(low)

    @pl.loop(0, groups)
    def _(c):
        for stage in range(4):
            sent_all(stage_routes(stage, c))
    sent_all(pair_routes())


def basis_kernel(mixer, sketch, basis):
    planes = basis.shape[1]
    k_all, _, ly, lz = sketch.shape
    tiles = ly // 8
    side = k_all * 8
    base = pl.program_id(0) * planes
    for i in range(planes):
        block = jnp.concatenate(
            [sketch[:, base + i, t * 8:t * 8 + 8, :].reshape(side, lz) for t in range(tiles)], axis=1
        )
        high = block.astype(jnp.bfloat16)
        low = (block - high.astype(jnp.float32)).astype(jnp.bfloat16)
        both = jnp.dot(
            mixer[...], jnp.concatenate([high, low], axis=0), preferred_element_type=jnp.float32
        )
        result = both[:side] + both[side:]
        for t in range(tiles):
            basis[:, i, t * 8:t * 8 + 8, :] = result[:, t * lz:(t + 1) * lz].reshape(k_all, 8, lz)


def local(nx, ny, directions, checkpoints, restart, diffusivity, velocity, weights):
    k_all, lx, ly, lz = directions.shape
    start = lax.dynamic_index_in_dim(checkpoints, restart[0], 0, keepdims=False)
    side = 8 * k_all
    groups = k_all // GROUP
    f32 = jnp.float32
    vmem = pl.BlockSpec(memory_space=pltpu.VMEM)
    anywhere = pl.BlockSpec(memory_space=pl.ANY)
    field = pltpu.VMEM((k_all, lx + 2, ly, lz), f32)
    cell = pltpu.VMEM((lx, ly, lz), f32)
    dma = pltpu.SemaphoreType.DMA
    sketch, mixer, factor = pl.pallas_call(
        functools.partial(sketch_kernel, nx, ny, float(nx * ny * lx * ly * lz)),
        out_shape=(
            pltpu.VMEM(directions.shape, f32),
            pltpu.VMEM((2 * side, 2 * side), jnp.bfloat16),
            jax.ShapeDtypeStruct((k_all, k_all), f32),
        ),
        in_specs=[pl.BlockSpec(memory_space=pltpu.SMEM)] + [anywhere] * 4,
        out_specs=(vmem, vmem, vmem),
        scratch_shapes=[
            field, field, field, field,
            pltpu.VMEM((2, lx + 2, ly, lz), f32),
            cell,
            pltpu.VMEM((6, lx, ly, lz), f32),
            pltpu.VMEM((6, lx, ly, lz), f32),
            cell, cell,
            pltpu.VMEM((4, 2, k_all, lx, lz), f32),
            pltpu.VMEM((4, 2, k_all, lx, lz), f32),
            pltpu.VMEM((2, 2, lx, lz), f32),
            pltpu.VMEM((2, 2, lx, lz), f32),
            pltpu.VMEM((nx, k_all, side), f32),
            pltpu.VMEM((ny, k_all, side), f32),
            dma((groups + 3,)),
            dma((4, 4, groups)),
            dma((4, 4, groups)),
            dma((4,)),
            dma((4,)),
            dma((nx + ny,)),
            dma((nx + ny,)),
        ],
        compiler_params=pltpu.CompilerParams(
            collective_id=0, has_side_effects=True, vmem_limit_bytes=48 * 2**20
        ),
        name="sketch",
    )(velocity, directions, start, diffusivity, weights)
    planes = 2
    basis = pl.pallas_call(
        basis_kernel,
        out_shape=jax.ShapeDtypeStruct(directions.shape, f32),
        grid=(lx // planes,),
        in_specs=[vmem, vmem],
        out_specs=pl.BlockSpec((k_all, planes, ly, lz), lambda i: (0, i, 0, 0)),
        compiler_params=pltpu.CompilerParams(vmem_limit_bytes=48 * 2**20),
        name="basis",
    )(mixer, sketch)
    return basis, factor


def solution(mesh):
    placed = (
        P(None, "gx", "gy", None),
        P(None, "gx", "gy", None),
        P(),
        P("gx", "gy", None),
        P(),
        P("gx", "gy", None),
    )
    return jax.shard_map(
        functools.partial(local, mesh.shape["gx"], mesh.shape["gy"]),
        mesh=mesh,
        in_specs=placed,
        out_specs=(P(None, "gx", "gy", None), P()),
        check_vma=False,
    )
```

```python
import functools

import jax
import jax.numpy as jnp
from jax import lax
from jax.experimental import pallas as pl
from jax.experimental.pallas import tpu as pltpu
from jax.sharding import PartitionSpec as P

DIFFUSE = 0.1
REACT = 0.05
PRIOR = 0.25
GROUP = 4
MESH = pl.DeviceIdType.MESH
HIGHEST = lax.Precision.HIGHEST


def iota(shape, dim):
    return lax.broadcasted_iota(jnp.int32, shape, dim)


def sketch_kernel(
    nx, ny, cells,
    velocity, restart, directions, checkpoints, diffusivity_in, weights_in,
    sketch, mixer, factor,
    f0, f1, f2, f3, pair, saved, wts, ct, ca, c0s, c0l,
    ysend, yrecv, ypsend, yprecv, gram_x, gram_y,
    local_sem, send_sem, recv_sem, psend_sem, precv_sem, gsend_sem, grecv_sem,
):
    fields = (f0, f1, f2, f3)
    k_all, lx, ly, lz = sketch.shape
    tiles = ly // 8
    groups = k_all // GROUP
    gx, gy = lax.axis_index("gx"), lax.axis_index("gy")

    barrier = pltpu.get_barrier_semaphore()
    for axis, me, count in (("gx", gx, nx), ("gy", gy, ny)):
        for step in range(1, count):
            pl.semaphore_signal(
                barrier, inc=1, device_id={axis: lax.rem(me + step, count)}, device_id_type=MESH
            )

    def load_group(c):
        ks = pl.ds(c * GROUP, GROUP)
        return pltpu.make_async_copy(
            directions.at[ks], f0.at[ks, pl.ds(1, lx)], local_sem.at[c]
        )

    side_copies = (
        pltpu.make_async_copy(checkpoints, saved, local_sem.at[groups]),
        pltpu.make_async_copy(diffusivity_in, pair.at[1, pl.ds(1, lx)], local_sem.at[groups + 1]),
        pltpu.make_async_copy(weights_in, wts, local_sem.at[groups + 2]),
    )
    load_group(0).start()
    side_copies[0].start()
    side_copies[1].start()
    side_copies[2].start()
    for c in range(1, groups):
        load_group(c).start()

    plane_zero = jnp.zeros((ly, lz), jnp.float32)
    row_zero = jnp.zeros((lx, lz), jnp.float32)

    for edge, where in ((gx == 0, 0), (gx == nx - 1, lx + 1)):
        @pl.when(edge)
        def _(where=where):
            @pl.loop(0, k_all)
            def _(k):
                for field in fields:
                    field[k, where] = plane_zero
            for k in range(2):
                pair[k, where] = plane_zero

    for edge, side in ((gy == 0, 0), (gy == ny - 1, 1)):
        @pl.when(edge)
        def _(side=side):
            @pl.loop(0, k_all)
            def _(k):
                for stage in range(4):
                    yrecv[stage, side, k] = row_zero
            for k in range(2):
                yprecv[side, k] = row_zero

    def routes(planes, ys, yr, ks, send, recv):
        def copy(src, dst, side, peer):
            return pltpu.make_async_remote_copy(
                src_ref=src, dst_ref=dst, send_sem=send(side), recv_sem=recv(side),
                device_id=peer, device_id_type=MESH,
            )
        return (
            (gx < nx - 1, gx > 0, copy(planes.at[ks, lx], planes.at[ks, 0], 0, {"gx": lax.rem(gx + 1, nx)})),
            (gx > 0, gx < nx - 1, copy(planes.at[ks, 1], planes.at[ks, lx + 1], 1, {"gx": lax.rem(gx + nx - 1, nx)})),
            (gy < ny - 1, gy > 0, copy(ys.at[0, ks], yr.at[0, ks], 2, {"gy": lax.rem(gy + 1, ny)})),
            (gy > 0, gy < ny - 1, copy(ys.at[1, ks], yr.at[1, ks], 3, {"gy": lax.rem(gy + ny - 1, ny)})),
        )

    def stage_routes(stage, c):
        return routes(
            fields[stage], ysend.at[stage], yrecv.at[stage], pl.ds(c * GROUP, GROUP),
            lambda side: send_sem.at[stage, side, c], lambda side: recv_sem.at[stage, side, c],
        )

    def pair_routes():
        return routes(
            pair, ypsend, yprecv, pl.ds(0, 2),
            lambda side: psend_sem.at[side], lambda side: precv_sem.at[side],
        )

    def send_all(ways):
        for sends, _, copy in ways:
            pl.when(sends)(copy.start)

    def recv_all(ways):
        for _, receives, copy in ways:
            pl.when(receives)(copy.wait_recv)

    def sent_all(ways):
        for sends, _, copy in ways:
            pl.when(sends)(copy.wait_send)

    row = iota((8, lz), 0)
    lane = iota((8, lz), 1)
    hx, hy, hz = (0.5 * velocity[i] for i in range(3))

    def around(field, yr, k, x, t):
        p = x + 1
        lo = t * 8
        middle = field[k, p, lo:lo + 8, :]
        east = field[k, p + 1, lo:lo + 8, :]
        west = field[k, p - 1, lo:lo + 8, :]
        if t < tiles - 1:
            north = field[k, p, lo + 1:lo + 9, :]
        else:
            north = jnp.where(row == 7, yr[1, k, pl.ds(x, 1), :], pltpu.roll(middle, 7, 0))
        if t > 0:
            south = field[k, p, lo - 1:lo + 7, :]
        else:
            south = jnp.where(row == 0, yr[0, k, pl.ds(x, 1), :], pltpu.roll(middle, 1, 0))
        upper = pltpu.roll(middle, lz - 1, 1)
        lower = pltpu.roll(middle, 1, 1)
        return middle, (east, west, north, south, upper, lower)

    def weighted(c0, cs, middle, sides):
        terms = [c * v for c, v in zip(cs, sides)]
        return ((terms[0] + terms[1]) + (terms[2] + terms[3])) + ((terms[4] + terms[5]) + c0 * middle)

    def pack_group(c):
        @pl.loop(0, lx)
        def _(x):
            for i in range(GROUP):
                k = c * GROUP + i
                ysend[0, 0, k, pl.ds(x, 1), :] = f0[k, x + 1, ly - 1:ly, :]
                ysend[0, 1, k, pl.ds(x, 1), :] = f0[k, x + 1, 0:1, :]

    load_group(0).wait()
    pack_group(0)
    side_copies[0].wait()
    side_copies[1].wait()

    first_state = restart[0]

    @pl.loop(0, lx)
    def _(x):
        pair[0, x + 1] = saved[first_state, x]
        for k in range(2):
            ypsend[0, k, pl.ds(x, 1), :] = pair[k, x + 1, ly - 1:ly, :]
            ypsend[1, k, pl.ds(x, 1), :] = pair[k, x + 1, 0:1, :]

    pl.semaphore_wait(barrier, nx + ny - 2)
    send_all(stage_routes(0, 0))
    send_all(pair_routes())

    @pl.loop(1, groups)
    def _(c):
        load_group(c).wait()
        pack_group(c)
        send_all(stage_routes(0, c))

    def run_stage(stage, coefs, centre, finish, out):
        field = fields[stage]
        last = stage == 3

        @pl.loop(0, groups)
        def _(c):
            recv_all(stage_routes(stage, c))

            @pl.loop(0, lx, unroll=8)
            def _(x):
                for t in range(tiles):
                    rows = slice(t * 8, t * 8 + 8)
                    cs = [coefs[i, x, rows, :] for i in range(6)]
                    c0 = centre[x, rows, :]
                    extra = wts[x, rows, :] if finish == "weights" else None
                    for i in range(GROUP):
                        k = c * GROUP + i
                        middle, sides = around(field, yrecv.at[stage], k, x, t)
                        value = weighted(c0, cs, middle, sides)
                        if finish == "weights":
                            value = extra * value
                        if finish == "prior":
                            value = value + PRIOR * f0[k, x + 1, rows, :]
                        if last:
                            out[k, x, rows, :] = value
                        else:
                            out[k, x + 1, rows, :] = value
                            if t == tiles - 1:
                                ysend[stage + 1, 0, k, pl.ds(x, 1), :] = value[7:8, :]
                            if t == 0:
                                ysend[stage + 1, 1, k, pl.ds(x, 1), :] = value[0:1, :]

            if not last:
                send_all(stage_routes(stage + 1, c))

    @pl.loop(0, lx)
    def _(x):
        for t in range(tiles):
            rows = slice(t * 8, t * 8 + 8)
            a = DIFFUSE * pair[1, x + 1, rows, :]
            state = pair[0, x + 1, rows, :]
            ct[0, x, rows, :] = a - hx
            ct[1, x, rows, :] = a + hx
            ct[2, x, rows, :] = a - hy
            ct[3, x, rows, :] = a + hy
            ct[4, x, rows, :] = jnp.where(lane < lz - 1, a - hz, 0.0)
            ct[5, x, rows, :] = jnp.where(lane > 0, a + hz, 0.0)
            c0s[x, rows, :] = 1.0 - 6.0 * a - (3.0 * REACT) * state * state

    run_stage(0, ct, c0s, None, f1)

    recv_all(pair_routes())
    side_copies[2].wait()

    @pl.loop(0, lx)
    def _(x):
        for t in range(tiles):
            rows = slice(t * 8, t * 8 + 8)
            state, sides = around(pair, yprecv, 0, x, t)
            cs = [ct[i, x, rows, :] for i in range(6)]
            diff, around_diff = around(pair, yprecv, 1, x, t)
            plain = 1.0 - (6.0 * DIFFUSE) * diff
            later = weighted(plain - REACT * state * state, cs, state, sides)
            c0l[x, rows, :] = plain - (3.0 * REACT) * later * later
            for i, (speed, other) in enumerate(zip((hx, -hx, hy, -hy, hz, -hz), around_diff)):
                value = DIFFUSE * other + speed
                if i == 4:
                    value = jnp.where(lane < lz - 1, value, 0.0)
                if i == 5:
                    value = jnp.where(lane > 0, value, 0.0)
                ca[i, x, rows, :] = value

    run_stage(1, ct, c0l, "weights", f2)
    run_stage(2, ca, c0l, None, f3)
    run_stage(3, ca, c0s, "prior", sketch)

    side = k_all * 8

    def products(x, total):
        block = jnp.concatenate(
            [sketch[:, x, t * 8:t * 8 + 8, :].reshape(side, lz) for t in range(tiles)], axis=1
        )
        high = block.astype(jnp.bfloat16)
        low = (block - high.astype(jnp.float32)).astype(jnp.bfloat16)
        return total + lax.dot_general(
            high, jnp.concatenate([high, low], axis=0), (((1,), (1,)), ((), ())),
            preferred_element_type=jnp.float32,
        )

    total = lax.fori_loop(0, lx, products, jnp.zeros((side, 2 * side), jnp.float32), unroll=4)
    low_part = total[:, side:]
    whole = total[:, :side] + low_part + low_part.T
    r_big, c_big = iota((side, side), 0), iota((side, side), 1)
    same_y = (r_big & 7) == (c_big & 7)
    whole = jnp.where(same_y, whole, 0.0)
    fold = (iota((k_all, side), 0) == iota((k_all, side), 1) >> 3).astype(jnp.float32)
    folded = jnp.dot(fold, whole, precision=HIGHEST, preferred_element_type=jnp.float32)

    for axis, me, count, slots, at in (("gx", gx, nx, gram_x, 0), ("gy", gy, ny, gram_y, nx)):
        slots[me] = folded
        copies = []
        for step in range(1, count):
            peer = lax.rem(me + step, count)
            copies.append(pltpu.make_async_remote_copy(
                src_ref=slots.at[me], dst_ref=slots.at[me],
                send_sem=gsend_sem.at[at + step], recv_sem=grecv_sem.at[at + me],
                device_id={axis: peer}, device_id_type=MESH,
            ))
        for copy in copies:
            copy.start()
        for step in range(1, count):
            peer = lax.rem(me + step, count)
            pltpu.make_async_remote_copy(
                src_ref=slots.at[peer], dst_ref=slots.at[peer],
                send_sem=gsend_sem.at[at + step], recv_sem=grecv_sem.at[at + peer],
                device_id={axis: peer}, device_id_type=MESH,
            ).wait_recv()
        folded = slots[0]
        for i in range(1, count):
            folded = folded + slots[i]
        for copy in copies:
            copy.wait_send()

    pick = (iota((side, lz), 0) >> 3 == iota((side, lz), 1)).astype(jnp.float32)
    work = jnp.dot(folded * (1.0 / cells), pick, precision=HIGHEST, preferred_element_type=jnp.float32)
    kr, kc = iota((k_all, lz), 0), iota((k_all, lz), 1)
    work = work + (kc == kr + k_all).astype(jnp.float32)
    for j in range(k_all - 1):
        ratio = jnp.where(kr > j, work[:, j:j + 1] / work[j:j + 1, j:j + 1], 0.0)
        work = work - ratio * work[j:j + 1, :]
    diagonal = jnp.sum(jnp.where(kr == kc, work, 0.0), axis=1, keepdims=True)
    work = work / jnp.sqrt(diagonal)
    factor[...] = jnp.where(kc >= kr, work, 0.0)[:, :k_all]
    spread = (iota((lz, side), 0) == (iota((lz, side), 1) >> 3) + k_all).astype(jnp.float32)
    inverse = jnp.dot(work, spread, precision=HIGHEST, preferred_element_type=jnp.float32)
    unfold = (iota((side, k_all), 0) >> 3 == iota((side, k_all), 1)).astype(jnp.float32)
    inverse = jnp.dot(unfold, inverse, precision=HIGHEST, preferred_element_type=jnp.float32)
    inverse = jnp.where(same_y, inverse, 0.0)
    high = inverse.astype(jnp.bfloat16)
    low = (inverse - high.astype(jnp.float32)).astype(jnp.bfloat16)
    mixer[:side, :side] = high
    mixer[:side, side:] = high
    mixer[side:, :side] = low
    mixer[side:, side:] = jnp.zeros_like(low)

    @pl.loop(0, groups)
    def _(c):
        for stage in range(4):
            sent_all(stage_routes(stage, c))
    sent_all(pair_routes())


def basis_kernel(mixer, sketch, basis):
    planes = basis.shape[1]
    k_all, _, ly, lz = sketch.shape
    tiles = ly // 8
    side = k_all * 8
    base = pl.program_id(0) * planes
    for i in range(planes):
        block = jnp.concatenate(
            [sketch[:, base + i, t * 8:t * 8 + 8, :].reshape(side, lz) for t in range(tiles)], axis=1
        )
        high = block.astype(jnp.bfloat16)
        low = (block - high.astype(jnp.float32)).astype(jnp.bfloat16)
        both = jnp.dot(
            mixer[...], jnp.concatenate([high, low], axis=0), preferred_element_type=jnp.float32
        )
        result = both[:side] + both[side:]
        for t in range(tiles):
            basis[:, i, t * 8:t * 8 + 8, :] = result[:, t * lz:(t + 1) * lz].reshape(k_all, 8, lz)


def local(nx, ny, directions, checkpoints, restart, diffusivity, velocity, weights):
    k_all, lx, ly, lz = directions.shape
    side = 8 * k_all
    groups = k_all // GROUP
    f32 = jnp.float32
    vmem = pl.BlockSpec(memory_space=pltpu.VMEM)
    scalars = pl.BlockSpec(memory_space=pltpu.SMEM)
    hbm = pl.BlockSpec(memory_space=pltpu.HBM)
    field = pltpu.VMEM((k_all, lx + 2, ly, lz), f32)
    cell = pltpu.VMEM((lx, ly, lz), f32)
    dma = pltpu.SemaphoreType.DMA
    sketch, mixer, factor = pl.pallas_call(
        functools.partial(sketch_kernel, nx, ny, float(nx * ny * lx * ly * lz)),
        out_shape=(
            pltpu.VMEM(directions.shape, f32),
            pltpu.VMEM((2 * side, 2 * side), jnp.bfloat16),
            jax.ShapeDtypeStruct((k_all, k_all), f32),
        ),
        in_specs=[scalars] * 2 + [hbm] * 4,
        out_specs=(vmem, vmem, vmem),
        scratch_shapes=[
            field, field, field, field,
            pltpu.VMEM((2, lx + 2, ly, lz), f32),
            pltpu.VMEM(checkpoints.shape, f32),
            cell,
            pltpu.VMEM((6, lx, ly, lz), f32),
            pltpu.VMEM((6, lx, ly, lz), f32),
            cell, cell,
            pltpu.VMEM((4, 2, k_all, lx, lz), f32),
            pltpu.VMEM((4, 2, k_all, lx, lz), f32),
            pltpu.VMEM((2, 2, lx, lz), f32),
            pltpu.VMEM((2, 2, lx, lz), f32),
            pltpu.VMEM((nx, k_all, side), f32),
            pltpu.VMEM((ny, k_all, side), f32),
            dma((groups + 3,)),
            dma((4, 4, groups)),
            dma((4, 4, groups)),
            dma((4,)),
            dma((4,)),
            dma((nx + ny,)),
            dma((nx + ny,)),
        ],
        compiler_params=pltpu.CompilerParams(
            collective_id=0, has_side_effects=True, vmem_limit_bytes=239 * 2**18
        ),
        name="sketch",
    )(velocity, restart, directions, checkpoints, diffusivity, weights)
    planes = 4
    basis = pl.pallas_call(
        basis_kernel,
        out_shape=jax.ShapeDtypeStruct(directions.shape, f32),
        grid=(lx // planes,),
        in_specs=[vmem, vmem],
        out_specs=pl.BlockSpec((k_all, planes, ly, lz), lambda i: (0, i, 0, 0)),
        compiler_params=pltpu.CompilerParams(vmem_limit_bytes=48 * 2**20),
        name="basis",
    )(mixer, sketch)
    return basis, factor


def solution(mesh):
    placed = (
        P(None, "gx", "gy", None),
        P(None, "gx", "gy", None),
        P(),
        P("gx", "gy", None),
        P(),
        P("gx", "gy", None),
    )
    return jax.shard_map(
        functools.partial(local, mesh.shape["gx"], mesh.shape["gy"]),
        mesh=mesh,
        in_specs=placed,
        out_specs=(P(None, "gx", "gy", None), P()),
        check_vma=False,
    )
```

```python
import functools

import jax
import jax.numpy as jnp
from jax import lax
from jax.experimental import pallas as pl
from jax.experimental.pallas import tpu as pltpu
from jax.sharding import PartitionSpec as P

DIFFUSE = 0.1
REACT = 0.05
PRIOR = 0.25
GROUP = 4
MESH = pl.DeviceIdType.MESH
HIGHEST = lax.Precision.HIGHEST


def iota(shape, dim):
    return lax.broadcasted_iota(jnp.int32, shape, dim)


def sketch_kernel(
    nx, ny, cells,
    velocity, restart, directions, checkpoints, diffusivity_in, weights_in,
    sketch, mixer, factor,
    f0, f1, f2, f3, pair, saved, wts, ct, ca, c0s, c0l,
    ysend, yrecv, ypsend, yprecv, gram_x, gram_y,
    local_sem, send_sem, recv_sem, psend_sem, precv_sem, gsend_sem, grecv_sem,
):
    fields = (f0, f1, f2, f3)
    k_all, lx, ly, lz = sketch.shape
    tiles = ly // 8
    groups = k_all // GROUP
    gx, gy = lax.axis_index("gx"), lax.axis_index("gy")

    barrier = pltpu.get_barrier_semaphore()
    for axis, me, count in (("gx", gx, nx), ("gy", gy, ny)):
        for step in range(1, count):
            pl.semaphore_signal(
                barrier, inc=1, device_id={axis: lax.rem(me + step, count)}, device_id_type=MESH
            )

    def load_group(c):
        ks = pl.ds(c * GROUP, GROUP)
        return pltpu.make_async_copy(
            directions.at[ks], f0.at[ks, pl.ds(1, lx)], local_sem.at[c]
        )

    side_copies = (
        pltpu.make_async_copy(checkpoints, saved, local_sem.at[groups]),
        pltpu.make_async_copy(diffusivity_in, pair.at[1, pl.ds(1, lx)], local_sem.at[groups + 1]),
        pltpu.make_async_copy(weights_in, wts, local_sem.at[groups + 2]),
    )
    for c in range(groups):
        load_group(c).start()
    for copy in (side_copies[1], side_copies[0], side_copies[2]):
        copy.start()

    plane_zero = jnp.zeros((ly, lz), jnp.float32)
    row_zero = jnp.zeros((lx, lz), jnp.float32)

    for edge, where in ((gx == 0, 0), (gx == nx - 1, lx + 1)):
        @pl.when(edge)
        def _(where=where):
            @pl.loop(0, k_all)
            def _(k):
                for field in fields:
                    field[k, where] = plane_zero
            for k in range(2):
                pair[k, where] = plane_zero

    for edge, side in ((gy == 0, 0), (gy == ny - 1, 1)):
        @pl.when(edge)
        def _(side=side):
            @pl.loop(0, k_all)
            def _(k):
                for stage in range(4):
                    yrecv[stage, side, k] = row_zero
            for k in range(2):
                yprecv[side, k] = row_zero

    def routes(planes, ys, yr, ks, send, recv):
        def copy(src, dst, side, peer):
            return pltpu.make_async_remote_copy(
                src_ref=src, dst_ref=dst, send_sem=send(side), recv_sem=recv(side),
                device_id=peer, device_id_type=MESH,
            )
        return (
            (gx < nx - 1, gx > 0, copy(planes.at[ks, lx], planes.at[ks, 0], 0, {"gx": lax.rem(gx + 1, nx)})),
            (gx > 0, gx < nx - 1, copy(planes.at[ks, 1], planes.at[ks, lx + 1], 1, {"gx": lax.rem(gx + nx - 1, nx)})),
            (gy < ny - 1, gy > 0, copy(ys.at[0, ks], yr.at[0, ks], 2, {"gy": lax.rem(gy + 1, ny)})),
            (gy > 0, gy < ny - 1, copy(ys.at[1, ks], yr.at[1, ks], 3, {"gy": lax.rem(gy + ny - 1, ny)})),
        )

    def stage_routes(stage, c):
        return routes(
            fields[stage], ysend.at[stage], yrecv.at[stage], pl.ds(c * GROUP, GROUP),
            lambda side: send_sem.at[stage, side, c], lambda side: recv_sem.at[stage, side, c],
        )

    def pair_routes():
        return routes(
            pair, ypsend, yprecv, pl.ds(0, 2),
            lambda side: psend_sem.at[side], lambda side: precv_sem.at[side],
        )

    def send_all(ways):
        for sends, _, copy in ways:
            pl.when(sends)(copy.start)

    def recv_all(ways):
        for _, receives, copy in ways:
            pl.when(receives)(copy.wait_recv)

    def sent_all(ways):
        for sends, _, copy in ways:
            pl.when(sends)(copy.wait_send)

    row = iota((8, lz), 0)
    lane = iota((8, lz), 1)
    hx, hy, hz = (0.5 * velocity[i] for i in range(3))

    def around(field, yr, k, x, t):
        p = x + 1
        lo = t * 8
        middle = field[k, p, lo:lo + 8, :]
        east = field[k, p + 1, lo:lo + 8, :]
        west = field[k, p - 1, lo:lo + 8, :]
        if t < tiles - 1:
            north = field[k, p, lo + 1:lo + 9, :]
        else:
            north = jnp.where(row == 7, yr[1, k, pl.ds(x, 1), :], pltpu.roll(middle, 7, 0))
        if t > 0:
            south = field[k, p, lo - 1:lo + 7, :]
        else:
            south = jnp.where(row == 0, yr[0, k, pl.ds(x, 1), :], pltpu.roll(middle, 1, 0))
        upper = pltpu.roll(middle, lz - 1, 1)
        lower = pltpu.roll(middle, 1, 1)
        return middle, (east, west, north, south, upper, lower)

    def weighted(c0, cs, middle, sides):
        terms = [c * v for c, v in zip(cs, sides)]
        return ((terms[0] + terms[1]) + (terms[2] + terms[3])) + ((terms[4] + terms[5]) + c0 * middle)

    def pack_group(c):
        @pl.loop(0, lx)
        def _(x):
            for i in range(GROUP):
                k = c * GROUP + i
                ysend[0, 0, k, pl.ds(x, 1), :] = f0[k, x + 1, ly - 1:ly, :]
                ysend[0, 1, k, pl.ds(x, 1), :] = f0[k, x + 1, 0:1, :]

    load_group(0).wait()
    pack_group(0)
    pl.semaphore_wait(barrier, nx + ny - 2)
    send_all(stage_routes(0, 0))

    @pl.loop(1, groups)
    def _(c):
        load_group(c).wait()
        pack_group(c)
        send_all(stage_routes(0, c))

    def run_stage(stage, coefs, centre, finish, out):
        field = fields[stage]
        last = stage == 3

        @pl.loop(0, groups)
        def _(c):
            recv_all(stage_routes(stage, c))

            @pl.loop(0, lx, unroll=8)
            def _(x):
                for t in range(tiles):
                    rows = slice(t * 8, t * 8 + 8)
                    cs = [coefs[i, x, rows, :] for i in range(6)]
                    c0 = centre[x, rows, :]
                    extra = wts[x, rows, :] if finish == "weights" else None
                    for i in range(GROUP):
                        k = c * GROUP + i
                        middle, sides = around(field, yrecv.at[stage], k, x, t)
                        value = weighted(c0, cs, middle, sides)
                        if finish == "weights":
                            value = extra * value
                        if finish == "prior":
                            value = value + PRIOR * f0[k, x + 1, rows, :]
                        if last:
                            out[k, x, rows, :] = value
                        else:
                            out[k, x + 1, rows, :] = value
                            if t == tiles - 1:
                                ysend[stage + 1, 0, k, pl.ds(x, 1), :] = value[7:8, :]
                            if t == 0:
                                ysend[stage + 1, 1, k, pl.ds(x, 1), :] = value[0:1, :]

            if not last:
                send_all(stage_routes(stage + 1, c))

    side_copies[0].wait()
    side_copies[1].wait()

    first_state = restart[0]

    @pl.loop(0, lx)
    def _(x):
        pair[0, x + 1] = saved[first_state, x]
        for k in range(2):
            ypsend[0, k, pl.ds(x, 1), :] = pair[k, x + 1, ly - 1:ly, :]
            ypsend[1, k, pl.ds(x, 1), :] = pair[k, x + 1, 0:1, :]

    send_all(pair_routes())

    @pl.loop(0, lx)
    def _(x):
        for t in range(tiles):
            rows = slice(t * 8, t * 8 + 8)
            a = DIFFUSE * pair[1, x + 1, rows, :]
            state = pair[0, x + 1, rows, :]
            ct[0, x, rows, :] = a - hx
            ct[1, x, rows, :] = a + hx
            ct[2, x, rows, :] = a - hy
            ct[3, x, rows, :] = a + hy
            ct[4, x, rows, :] = jnp.where(lane < lz - 1, a - hz, 0.0)
            ct[5, x, rows, :] = jnp.where(lane > 0, a + hz, 0.0)
            c0s[x, rows, :] = 1.0 - 6.0 * a - (3.0 * REACT) * state * state

    run_stage(0, ct, c0s, None, f1)

    recv_all(pair_routes())
    side_copies[2].wait()

    @pl.loop(0, lx)
    def _(x):
        for t in range(tiles):
            rows = slice(t * 8, t * 8 + 8)
            state, sides = around(pair, yprecv, 0, x, t)
            cs = [ct[i, x, rows, :] for i in range(6)]
            diff, around_diff = around(pair, yprecv, 1, x, t)
            plain = 1.0 - (6.0 * DIFFUSE) * diff
            later = weighted(plain - REACT * state * state, cs, state, sides)
            c0l[x, rows, :] = plain - (3.0 * REACT) * later * later
            for i, (speed, other) in enumerate(zip((hx, -hx, hy, -hy, hz, -hz), around_diff)):
                value = DIFFUSE * other + speed
                if i == 4:
                    value = jnp.where(lane < lz - 1, value, 0.0)
                if i == 5:
                    value = jnp.where(lane > 0, value, 0.0)
                ca[i, x, rows, :] = value

    run_stage(1, ct, c0l, "weights", f2)
    run_stage(2, ca, c0l, None, f3)
    run_stage(3, ca, c0s, "prior", sketch)

    side = k_all * 8

    def products(x, total):
        block = jnp.concatenate(
            [sketch[:, x, t * 8:t * 8 + 8, :].reshape(side, lz) for t in range(tiles)], axis=1
        )
        high = block.astype(jnp.bfloat16)
        low = (block - high.astype(jnp.float32)).astype(jnp.bfloat16)
        return total + lax.dot_general(
            high, jnp.concatenate([high, low], axis=0), (((1,), (1,)), ((), ())),
            preferred_element_type=jnp.float32,
        )

    total = lax.fori_loop(0, lx, products, jnp.zeros((side, 2 * side), jnp.float32), unroll=4)
    low_part = total[:, side:]
    whole = total[:, :side] + low_part + low_part.T
    r_big, c_big = iota((side, side), 0), iota((side, side), 1)
    same_y = (r_big & 7) == (c_big & 7)
    whole = jnp.where(same_y, whole, 0.0)
    fold = (iota((k_all, side), 0) == iota((k_all, side), 1) >> 3).astype(jnp.float32)
    folded = jnp.dot(fold, whole, precision=HIGHEST, preferred_element_type=jnp.float32)

    for axis, me, count, slots, at in (("gx", gx, nx, gram_x, 0), ("gy", gy, ny, gram_y, nx)):
        slots[me] = folded
        copies = []
        for step in range(1, count):
            peer = lax.rem(me + step, count)
            copies.append(pltpu.make_async_remote_copy(
                src_ref=slots.at[me], dst_ref=slots.at[me],
                send_sem=gsend_sem.at[at + step], recv_sem=grecv_sem.at[at + me],
                device_id={axis: peer}, device_id_type=MESH,
            ))
        for copy in copies:
            copy.start()
        for step in range(1, count):
            peer = lax.rem(me + step, count)
            pltpu.make_async_remote_copy(
                src_ref=slots.at[peer], dst_ref=slots.at[peer],
                send_sem=gsend_sem.at[at + step], recv_sem=grecv_sem.at[at + peer],
                device_id={axis: peer}, device_id_type=MESH,
            ).wait_recv()
        folded = slots[0]
        for i in range(1, count):
            folded = folded + slots[i]
        for copy in copies:
            copy.wait_send()

    pick = (iota((side, lz), 0) >> 3 == iota((side, lz), 1)).astype(jnp.float32)
    work = jnp.dot(folded * (1.0 / cells), pick, precision=HIGHEST, preferred_element_type=jnp.float32)
    kr, kc = iota((k_all, lz), 0), iota((k_all, lz), 1)
    work = work + (kc == kr + k_all).astype(jnp.float32)
    for j in range(k_all - 1):
        ratio = jnp.where(kr > j, work[:, j:j + 1] / work[j:j + 1, j:j + 1], 0.0)
        work = work - ratio * work[j:j + 1, :]
    diagonal = jnp.sum(jnp.where(kr == kc, work, 0.0), axis=1, keepdims=True)
    work = work / jnp.sqrt(diagonal)
    factor[...] = jnp.where(kc >= kr, work, 0.0)[:, :k_all]
    spread = (iota((lz, side), 0) == (iota((lz, side), 1) >> 3) + k_all).astype(jnp.float32)
    inverse = jnp.dot(work, spread, precision=HIGHEST, preferred_element_type=jnp.float32)
    unfold = (iota((side, k_all), 0) >> 3 == iota((side, k_all), 1)).astype(jnp.float32)
    inverse = jnp.dot(unfold, inverse, precision=HIGHEST, preferred_element_type=jnp.float32)
    inverse = jnp.where(same_y, inverse, 0.0)
    high = inverse.astype(jnp.bfloat16)
    low = (inverse - high.astype(jnp.float32)).astype(jnp.bfloat16)
    mixer[:side, :side] = high
    mixer[:side, side:] = high
    mixer[side:, :side] = low
    mixer[side:, side:] = jnp.zeros_like(low)

    @pl.loop(0, groups)
    def _(c):
        for stage in range(4):
            sent_all(stage_routes(stage, c))
    sent_all(pair_routes())


def basis_kernel(mixer, sketch, basis):
    planes = basis.shape[1]
    k_all, _, ly, lz = sketch.shape
    tiles = ly // 8
    side = k_all * 8
    base = pl.program_id(0) * planes
    for i in range(planes):
        block = jnp.concatenate(
            [sketch[:, base + i, t * 8:t * 8 + 8, :].reshape(side, lz) for t in range(tiles)], axis=1
        )
        high = block.astype(jnp.bfloat16)
        low = (block - high.astype(jnp.float32)).astype(jnp.bfloat16)
        both = jnp.dot(
            mixer[...], jnp.concatenate([high, low], axis=0), preferred_element_type=jnp.float32
        )
        result = both[:side] + both[side:]
        for t in range(tiles):
            basis[:, i, t * 8:t * 8 + 8, :] = result[:, t * lz:(t + 1) * lz].reshape(k_all, 8, lz)


def local(nx, ny, directions, checkpoints, restart, diffusivity, velocity, weights):
    k_all, lx, ly, lz = directions.shape
    side = 8 * k_all
    groups = k_all // GROUP
    f32 = jnp.float32
    vmem = pl.BlockSpec(memory_space=pltpu.VMEM)
    scalars = pl.BlockSpec(memory_space=pltpu.SMEM)
    hbm = pl.BlockSpec(memory_space=pltpu.HBM)
    field = pltpu.VMEM((k_all, lx + 2, ly, lz), f32)
    cell = pltpu.VMEM((lx, ly, lz), f32)
    dma = pltpu.SemaphoreType.DMA
    sketch, mixer, factor = pl.pallas_call(
        functools.partial(sketch_kernel, nx, ny, float(nx * ny * lx * ly * lz)),
        out_shape=(
            pltpu.VMEM(directions.shape, f32),
            pltpu.VMEM((2 * side, 2 * side), jnp.bfloat16),
            jax.ShapeDtypeStruct((k_all, k_all), f32),
        ),
        in_specs=[scalars] * 2 + [hbm] * 4,
        out_specs=(vmem, vmem, vmem),
        scratch_shapes=[
            field, field, field, field,
            pltpu.VMEM((2, lx + 2, ly, lz), f32),
            pltpu.VMEM(checkpoints.shape, f32),
            cell,
            pltpu.VMEM((6, lx, ly, lz), f32),
            pltpu.VMEM((6, lx, ly, lz), f32),
            cell, cell,
            pltpu.VMEM((4, 2, k_all, lx, lz), f32),
            pltpu.VMEM((4, 2, k_all, lx, lz), f32),
            pltpu.VMEM((2, 2, lx, lz), f32),
            pltpu.VMEM((2, 2, lx, lz), f32),
            pltpu.VMEM((nx, k_all, side), f32),
            pltpu.VMEM((ny, k_all, side), f32),
            dma((groups + 3,)),
            dma((4, 4, groups)),
            dma((4, 4, groups)),
            dma((4,)),
            dma((4,)),
            dma((nx + ny,)),
            dma((nx + ny,)),
        ],
        compiler_params=pltpu.CompilerParams(
            collective_id=0, has_side_effects=True, vmem_limit_bytes=239 * 2**18
        ),
        name="sketch",
    )(velocity, restart, directions, checkpoints, diffusivity, weights)
    planes = 4
    basis = pl.pallas_call(
        basis_kernel,
        out_shape=jax.ShapeDtypeStruct(directions.shape, f32),
        grid=(lx // planes,),
        in_specs=[vmem, vmem],
        out_specs=pl.BlockSpec((k_all, planes, ly, lz), lambda i: (0, i, 0, 0)),
        compiler_params=pltpu.CompilerParams(vmem_limit_bytes=48 * 2**20),
        name="basis",
    )(mixer, sketch)
    return basis, factor


def solution(mesh):
    placed = (
        P(None, "gx", "gy", None),
        P(None, "gx", "gy", None),
        P(),
        P("gx", "gy", None),
        P(),
        P("gx", "gy", None),
    )
    return jax.shard_map(
        functools.partial(local, mesh.shape["gx"], mesh.shape["gy"]),
        mesh=mesh,
        in_specs=placed,
        out_specs=(P(None, "gx", "gy", None), P()),
        check_vma=False,
    )
```
